256 devices in a mesh: cfg: 2 (over y_lo), blk: 32 (over y_hi, z, core), uly: 4 (over x).
Axes of the slice: x: 4, y: 4 (y_hi: 2, y_lo: 2; y = y_hi * 2 + y_lo), z: 8, core: 2. Of those that a mesh axis runs over, the one named last changes fastest.
Arguments:
- query: bfloat16 [2, 8192, 2048], P('cfg', ('blk', 'uly')), may hold values from -6 to 6
- key: bfloat16 [2, 8192, 2048], P('cfg', ('blk', 'uly')), may hold values from -6 to 6
- value: bfloat16 [2, 8192, 2048], P('cfg', ('blk', 'uly')), may hold values from -6 to 6
- text_key: bfloat16 [2, 333, 2048], P('cfg'), may hold values from -6 to 6
- text_value: bfloat16 [2, 333, 2048], P('cfg'), may hold values from -6 to 6
- stream: bfloat16 [2, 8192, 2432], P('cfg', ('blk', 'uly')), may hold values from -30 to 30
- modulation: float32 [2, 5, 2432], P('cfg'), may hold values from -3 to 3
- out_weight: bfloat16 [2048, 2432], P(('uly', 'blk')), may hold values from -0.125 to 0.125
- final_weight: bfloat16 [2432, 64], replicated, may hold values from -0.125 to 0.125
- final_bias: float32 [64], replicated, may hold values from -3 to 3
- latents: float32 [8192, 64], P(('blk', 'uly')), may hold values from -5 to 5
- sigmas: float32 [29], replicated, may hold values from 0 to 1, as said below
- step_index: int32 [1], replicated, may hold values from 0 to 27
- patch_weight: bfloat16 [64, 2432], replicated, may hold values from -0.75 to 0.75
- position: bfloat16 [8192, 2432], P('blk'), may hold values from -1 to 1
- qkv_weight: bfloat16 [3, 2432, 2048], P(None, 'blk', 'uly'), may hold values from -0.125 to 0.125
- norm_gains: float32 [2, 64], replicated, may hold values from 0.25 to 1.75
Outputs:
- velocity: float32 [8192, 64], P(('blk', 'uly'))
- latents_next: float32 [8192, 64], P(('blk', 'uly'))
- next_qkv: bfloat16 [2, 3, 8192, 2048], P('cfg', None, 'blk', 'uly')
The draws below stay inside these ranges and needn't reach their ends.
Inputs may be any that keep to these rules, and one draw needn't show every extreme that they name: Decreasing, with sigmas[0] = 1 and sigmas[28] = 0.
All inputs are finite; a program needn't handle non-finite values.
Results may differ from the reference program's by a relative error of at most 0.013.
Values may be sent and summed in bfloat16 or wider, within the bound.
No kernel may reach another device: no remote copies, remote signals or barrier semaphores. Data moves between devices by JAX's collectives and lax.ppermute only.
A program may use at most 128 MiB of HBM per device.

```python
import jax
import jax.numpy as jnp
from jax import lax

D = 2432
HD = 64
HEADS = 32
CH = 64
TXT = 333
STEPS = 28
IMG = 8192
AI = 2048


def draw_query(key, part):
    key = jax.random.fold_in(key, 1)
    base = jnp.clip(1.8 * jax.random.normal(key, (2, IMG, AI), jnp.float32), -6.0, 6.0)
    return base.astype(jnp.bfloat16)


def draw_key(key, part):
    key = jax.random.fold_in(key, 2)
    base = jnp.clip(1.8 * jax.random.normal(key, (2, IMG, AI), jnp.float32), -6.0, 6.0)
    return base.astype(jnp.bfloat16)


def draw_stream(key, part):
    key = jax.random.fold_in(key, 11)
    first = jax.random.fold_in(key, 0)
    fourth = jax.random.fold_in(key, 3)
    columns = jnp.exp(jax.random.uniform(first, (D,), jnp.float32, 0.0, 2.302585))
    base = jnp.clip(jax.random.normal(fourth, (2, IMG, D), jnp.float32), -4.0, 4.0)
    return (0.3 * columns * base).astype(jnp.bfloat16)


def draw_sigmas(key, part):
    key = jax.random.fold_in(key, 7)
    first, second = jax.random.split(key, 2)
    shift = jnp.exp(jax.random.uniform(first, (), jnp.float32, 0.182322, 2.079442))
    jitter = jax.random.uniform(second, (STEPS + 1,), jnp.float32, -0.45, 0.45) / STEPS
    places = jnp.arange(STEPS + 1).astype(jnp.float32)
    inside = (places > 0) & (places < STEPS)
    level = 1.0 - places / STEPS + jnp.where(inside, jitter, 0.0)
    return shift * level / (1.0 + (shift - 1.0) * level)


def steps_of(key, shape, cuts, smallest, largest):
    level, own = 1.0, jax.random.fold_in(key, 6)
    for dim, parts in cuts:
        heights = jnp.exp(jax.random.uniform(jax.random.fold_in(own, dim), (parts,), jnp.float32, smallest / len(cuts), largest / len(cuts)))
        level = level * jnp.repeat(heights, shape[dim] // parts).reshape([-1 if axis == dim else 1 for axis in range(len(shape))])
    return level


def noise(stream_key, dims, deviation, limit, cuts=(), held_as=jnp.bfloat16):
    drawn = jax.random.normal(stream_key, dims, jnp.float32) * deviation
    if len(cuts) > 0:
        drawn = steps_of(stream_key, dims, cuts, -0.22, 0.18) * drawn
    return jnp.clip(drawn, min=-limit, max=limit).astype(held_as)


def setup_inputs(seed: int = 0) -> dict:
    streams_of = jax.random.split(jax.random.key(seed), 18)
    query = draw_query(jax.random.fold_in(streams_of[17], 71), 0)
    key = draw_key(jax.random.fold_in(streams_of[17], 71), 0)
    value = noise(streams_of[2], (2, IMG, AI), 1.0, 6.0, ((0, 2), (1, 128)))
    text_key = noise(streams_of[3], (2, TXT, AI), 1.8, 6.0, ((0, 2),))
    text_value = noise(streams_of[4], (2, TXT, AI), 1.0, 6.0, ((0, 2),))
    stream = draw_stream(jax.random.fold_in(streams_of[17], 71), 0)
    modulation = noise(streams_of[6], (2, 5, D), 0.5, 3.0, ((0, 2),), jnp.float32)
    out_weight = noise(streams_of[7], (AI, D), AI ** -0.5, 0.125, ((0, 128),))
    final_weight = noise(streams_of[8], (D, CH), D ** -0.5, 0.125)
    final_bias = noise(streams_of[9], (CH,), 0.5, 3.0, (), jnp.float32)
    latents = noise(streams_of[10], (IMG, CH), 1.0, 5.0, ((0, 128),), jnp.float32)
    sigmas = draw_sigmas(jax.random.fold_in(streams_of[17], 71), 0)
    step_index = jax.random.randint(streams_of[12], (1,), 0, STEPS).astype(jnp.int32)
    patch_weight = noise(streams_of[13], (CH, D), CH ** -0.5, 0.75)
    position = jnp.clip(jax.random.uniform(streams_of[14], (IMG, D), jnp.float32, -1.0, 1.0) * steps_of(streams_of[14], (IMG, D), ((0, 32),), -0.4, 0.0), -1.0, 1.0).astype(jnp.bfloat16)
    qkv_weight = noise(streams_of[15], (3, D, AI), D ** -0.5, 0.125, ((1, 32), (2, 4)))
    norm_gains = jnp.clip(1.0 + 0.15 * jax.random.normal(streams_of[16], (2, HD), jnp.float32), 0.25, 1.75)
    return dict(query=query, key=key, value=value, text_key=text_key, text_value=text_value, stream=stream, modulation=modulation, out_weight=out_weight, final_weight=final_weight, final_bias=final_bias, latents=latents, sigmas=sigmas, step_index=step_index, patch_weight=patch_weight, position=position, qkv_weight=qkv_weight, norm_gains=norm_gains)


norm_epsilon = 1e-06
guidance_scale = 3.5

def layer_norm(matrix):
    mean = lax.optimization_barrier(jnp.mean(matrix, axis=-1, keepdims=True))
    centred = matrix - mean
    variance = lax.optimization_barrier(jnp.mean(centred * centred, axis=-1, keepdims=True))
    return centred * lax.rsqrt(variance + norm_epsilon)

def head_rms(matrix, gain):
    height = matrix.shape[0]
    shaped = matrix.reshape(height, -1, HD)
    squares = lax.optimization_barrier(jnp.mean(shaped * shaped, axis=-1, keepdims=True))
    return (shaped * lax.rsqrt(squares + norm_epsilon) * gain).reshape(height, -1)

def attend(query, key, value, text_key, text_value):
    keys_all = jnp.concatenate([key, text_key], axis=0)
    values_all = jnp.concatenate([value, text_value], axis=0)
    head_queries = query.reshape(IMG, HEADS, HD).transpose(1, 0, 2)
    head_keys = keys_all.reshape(-1, HEADS, HD).transpose(1, 0, 2)
    head_values = values_all.reshape(-1, HEADS, HD).transpose(1, 0, 2)

    def one_head(operands):
        single_query, single_keys, single_values = operands
        scores = jnp.dot(single_query, single_keys.T, preferred_element_type=jnp.float32) * HD ** (-0.5)
        peak = lax.optimization_barrier(jnp.max(scores, axis=-1, keepdims=True))
        expo = jnp.exp(scores - peak)
        total = lax.optimization_barrier(jnp.sum(expo, axis=-1, keepdims=True))
        mixed = jnp.dot(expo.astype(jnp.bfloat16), single_values, preferred_element_type=jnp.float32) / total
        return mixed.astype(jnp.bfloat16)
    outputs = lax.map(one_head, (head_queries, head_keys, head_values))
    return outputs.transpose(1, 0, 2).reshape(IMG, HEADS * HD)

def reference(query, key, value, text_key, text_value, stream, modulation, out_weight, final_weight, final_bias, latents, sigmas, step_index, patch_weight, position, qkv_weight, norm_gains):
    predictions = []
    for branch in range(2):
        attended = attend(query[branch], key[branch], value[branch], text_key[branch], text_value[branch])
        projected = jnp.dot(attended, out_weight, preferred_element_type=jnp.float32)
        params = modulation[branch]
        residual = stream[branch].astype(jnp.float32) + params[0] * projected
        normed = (layer_norm(residual) * (1.0 + params[2]) + params[1]).astype(jnp.bfloat16)
        predictions.append(jnp.dot(normed, final_weight, preferred_element_type=jnp.float32) + final_bias)
    velocity = predictions[1] + guidance_scale * (predictions[0] - predictions[1])
    moment = step_index[0]
    latents_next = latents + (sigmas[moment + 1] - sigmas[moment]) * velocity
    latents_low = latents_next.astype(jnp.bfloat16)
    embedded = jnp.dot(latents_low, patch_weight, preferred_element_type=jnp.float32) + position.astype(jnp.float32)
    base_norm = layer_norm(embedded)
    results = []
    for branch in range(2):
        params = modulation[branch]
        inputs = (base_norm * (1.0 + params[4]) + params[3]).astype(jnp.bfloat16)
        next_query = head_rms(jnp.dot(inputs, qkv_weight[0], preferred_element_type=jnp.float32), norm_gains[0])
        next_key = head_rms(jnp.dot(inputs, qkv_weight[1], preferred_element_type=jnp.float32), norm_gains[1])
        next_value = jnp.dot(inputs, qkv_weight[2], preferred_element_type=jnp.float32)
        results.append(jnp.stack([next_query, next_key, next_value]).astype(jnp.bfloat16))
    return (velocity, latents_next, jnp.stack(results))
```

```python
import functools

import jax
import jax.numpy as jnp
from jax import lax
from jax.experimental import pallas as pl
from jax.experimental.pallas import tpu as pltpu
from jax.sharding import Mesh, PartitionSpec as P

HD = 64
norm_epsilon = 1e-06
guidance_scale = 3.5
bf16 = jnp.bfloat16
f32 = jnp.float32
KEY_BLOCK = 1024


def params(limit_mib=56, **more):
    return pltpu.CompilerParams(vmem_limit_bytes=limit_mib * 2**20, **more)


def whole(shape):
    return pl.BlockSpec(shape, lambda *_: (0,) * len(shape))


def half_swap(block):
    return pltpu.roll(block.astype(f32), 64, 1).astype(block.dtype)


def low_lanes(shape):
    return lax.broadcasted_iota(jnp.int32, shape, len(shape) - 1) < 64


def pack_kernel(zs, us, head_ref, query_ref, key_ref, value_ref, text_key_ref, text_value_ref, send_ref, text_ref):
    rows = query_ref.shape[1]
    half = rows // 2
    low = low_lanes((rows, 128))
    low_half = low_lanes((half, 128))
    for pair in range(zs * us // 2):
        lanes = slice(128 * pair, 128 * pair + 128)
        keys = key_ref[0, :, lanes]
        values = value_ref[0, :, lanes]
        queries = query_ref[0, :, lanes] * 0.125
        first, second = queries[:half], queries[half:]
        for odd in range(2):
            head = 2 * pair + odd
            place = (head % zs) * us + head // zs
            if odd:
                both = jnp.where(low, half_swap(keys), values)
                folded = jnp.where(low_half, half_swap(first), second)
            else:
                both = jnp.where(low, keys, half_swap(values))
                folded = jnp.where(low_half, first, half_swap(second))
            send_ref[place, :rows, :] = both
            send_ref[place, rows:, :] = folded
    odd_head = lax.rem(head_ref[0], 2) == 1
    text_rows = text_key_ref.shape[1]
    text_low = low_lanes((text_rows, 128))
    keys = text_key_ref[0]
    values = text_value_ref[0]
    both = jnp.where(
        text_low,
        jnp.where(odd_head, half_swap(keys), keys),
        jnp.where(odd_head, values, half_swap(values)),
    )
    text_ref[...] = jnp.zeros(text_ref.shape, bf16)
    text_ref[:text_rows, :] = both


def pack(zs, us, head, query, key, value, text_key, text_value):
    rows = query.shape[1]
    text_rows = text_key.shape[1]
    text_padded = -(-text_rows // 128) * 128
    text_spec = pl.BlockSpec((1, text_rows, 128), lambda i, head: (0, 0, head[0] // 2))
    return pl.pallas_call(
        functools.partial(pack_kernel, zs, us),
        grid_spec=pltpu.PrefetchScalarGridSpec(
            num_scalar_prefetch=1,
            grid=(1,),
            in_specs=[whole(query.shape), whole(key.shape), whole(value.shape), text_spec, text_spec],
            out_specs=[whole((zs * us, rows + rows // 2, 128)), whole((text_padded, 128))],
        ),
        out_shape=[
            jax.ShapeDtypeStruct((zs * us, rows + rows // 2, 128), bf16),
            jax.ShapeDtypeStruct((text_padded, 128), bf16),
        ],
        compiler_params=params(),
        name="pack",
    )(head, query, key, value, text_key, text_value)


def value_rows(both):
    return jnp.concatenate([jnp.transpose(both)[64:], jnp.ones((16, both.shape[0]), bf16)], axis=0)


def scores_of(both, queries):
    return lax.dot_general(both, queries, (((1,), (1,)), ((), ())), preferred_element_type=f32)


def fold(peak, mixed, both, queries):
    scores = scores_of(both, queries)
    new_peak = jnp.maximum(peak, jnp.max(scores, axis=0, keepdims=True))
    weights = jnp.exp(scores - new_peak).astype(bf16)
    mixed = mixed * jnp.exp(peak - new_peak) + jnp.dot(value_rows(both), weights, preferred_element_type=f32)
    return new_peak, mixed


def first_kernel(text_count, pieces_ref, text_ref, both_ref, queries_ref, peak_ref, mixed_ref):
    step = pl.program_id(0)

    @pl.when(step == 0)
    def _():
        count, height, _ = pieces_ref.shape
        half = height // 3
        folded = pieces_ref[:, 2 * half :, :].reshape(count * half, 128)
        low = low_lanes(folded.shape)
        zero = jnp.zeros_like(folded)
        first = jnp.where(low, folded, zero).reshape(count, half, 128)
        second = jnp.where(low, half_swap(folded), zero).reshape(count, half, 128)
        queries = jnp.concatenate([first, second], axis=1).reshape(count * 2 * half, 128)
        queries_ref[...] = queries
        text = text_ref[...]
        scores = scores_of(text, queries)
        kept = lax.broadcasted_iota(jnp.int32, scores.shape, 0) < text_count
        scores = jnp.where(kept, scores, -1e30)
        peak = jnp.max(scores, axis=0, keepdims=True)
        weights = jnp.exp(scores - peak).astype(bf16)
        peak_ref[...] = peak
        mixed_ref[...] = jnp.dot(value_rows(text), weights, preferred_element_type=f32)

    peak_ref[...], mixed_ref[...] = fold(peak_ref[...], mixed_ref[...], both_ref[...], queries_ref[...])


def first_attend(text_count, pieces, text, both):
    count, height, _ = pieces.shape
    total = count * (height // 3) * 2
    return pl.pallas_call(
        functools.partial(first_kernel, text_count),
        grid=(both.shape[0] // KEY_BLOCK,),
        in_specs=[whole(pieces.shape), whole(text.shape), pl.BlockSpec((KEY_BLOCK, 128), lambda i: (i, 0))],
        out_specs=[whole((total, 128)), whole((1, total)), whole((80, total))],
        out_shape=[
            jax.ShapeDtypeStruct((total, 128), bf16),
            jax.ShapeDtypeStruct((1, total), f32),
            jax.ShapeDtypeStruct((80, total), f32),
        ],
        compiler_params=params(),
        name="attend_first",
    )(pieces, text, both)


def next_kernel(queries_ref, peak_in_ref, mixed_in_ref, both_ref, peak_ref, mixed_ref):
    @pl.when(pl.program_id(0) == 0)
    def _():
        peak_ref[...] = peak_in_ref[...]
        mixed_ref[...] = mixed_in_ref[...]

    peak_ref[...], mixed_ref[...] = fold(peak_ref[...], mixed_ref[...], both_ref[...], queries_ref[...])


def next_attend(queries, peak, mixed, both):
    return pl.pallas_call(
        next_kernel,
        grid=(both.shape[0] // KEY_BLOCK,),
        in_specs=[
            whole(queries.shape),
            whole(peak.shape),
            whole(mixed.shape),
            pl.BlockSpec((KEY_BLOCK, 128), lambda i: (i, 0)),
        ],
        out_specs=[whole(peak.shape), whole(mixed.shape)],
        out_shape=[jax.ShapeDtypeStruct(peak.shape, f32), jax.ShapeDtypeStruct(mixed.shape, f32)],
        compiler_params=params(),
        name="attend_next",
    )(queries, peak, mixed, both)


def last_kernel(steps, queries_ref, peak_in_ref, mixed_in_ref, one_ref, two_ref, out_ref, peak_ref, mixed_ref):
    step = pl.program_id(0)

    @pl.when(step == 0)
    def _():
        peak_ref[...] = peak_in_ref[...]
        mixed_ref[...] = mixed_in_ref[...]

    both = jnp.where(step < steps, one_ref[...], two_ref[...])
    peak_ref[...], mixed_ref[...] = fold(peak_ref[...], mixed_ref[...], both, queries_ref[...])

    @pl.when(step == 2 * steps - 1)
    def _():
        mixed = mixed_ref[...]
        attended = (mixed[:64] / mixed[64:65]).astype(bf16)
        width = out_ref.shape[2]
        for place in range(out_ref.shape[0]):
            out_ref[place] = attended[:, place * width : place * width + width]


def last_attend(zs, queries, peak, mixed, one, two):
    steps = one.shape[0] // KEY_BLOCK
    total = queries.shape[0]
    return pl.pallas_call(
        functools.partial(last_kernel, steps),
        grid=(2 * steps,),
        in_specs=[
            whole(queries.shape),
            whole(peak.shape),
            whole(mixed.shape),
            pl.BlockSpec((KEY_BLOCK, 128), lambda i: (jnp.minimum(i, steps - 1), 0)),
            pl.BlockSpec((KEY_BLOCK, 128), lambda i: (jnp.maximum(i - steps, 0), 0)),
        ],
        out_specs=whole((zs, 64, total // zs)),
        out_shape=jax.ShapeDtypeStruct((zs, 64, total // zs), bf16),
        scratch_shapes=[pltpu.VMEM(peak.shape, f32), pltpu.VMEM(mixed.shape, f32)],
        compiler_params=params(),
        name="attend_last",
    )(queries, peak, mixed, one, two)


def project_kernel(place_ref, attended_ref, weight_ref, *refs):
    outs, held = refs[:-1], refs[-1]
    heads, _, tokens = attended_ref.shape
    attended = jnp.transpose(attended_ref[...].reshape(heads * 64, tokens))
    slabs, sides, rows, width = weight_ref.shape
    depth = slabs * rows
    total = jnp.zeros((tokens, width), f32)
    for side in range(sides):
        part = weight_ref[:, side].reshape(depth, width)
        total += jnp.dot(attended[:, side * depth : side * depth + depth], part, preferred_element_type=f32)
    held[...] = total.astype(bf16)
    count = len(outs)
    size = tokens // count
    for step, out_ref in enumerate(outs):
        start = pl.multiple_of(lax.rem(place_ref[0] + step, count) * size, size)
        out_ref[...] = held[pl.ds(start, size), :]


def project(us, place, attended, weight):
    tokens = attended.shape[2]
    width = weight.shape[-1]
    piece = (tokens // us, width)
    return pl.pallas_call(
        project_kernel,
        grid_spec=pltpu.PrefetchScalarGridSpec(
            num_scalar_prefetch=1,
            grid=(1,),
            in_specs=[whole(attended.shape), whole(weight.shape)],
            out_specs=[whole(piece)] * us,
            scratch_shapes=[pltpu.VMEM((tokens, width), bf16)],
        ),
        out_shape=[jax.ShapeDtypeStruct(piece, bf16)] * us,
        compiler_params=params(),
        name="project",
    )(place, attended, weight)


def layer_norm(matrix):
    mean = jnp.mean(matrix, axis=-1, keepdims=True)
    centred = matrix - mean
    variance = jnp.mean(centred * centred, axis=-1, keepdims=True)
    return centred * lax.rsqrt(variance + norm_epsilon)


def predict_kernel(stream_ref, modulation_ref, weight_ref, bias_ref, *refs):
    pieces, out_ref = refs[:-1], refs[-1]
    projected = pieces[0][...].astype(f32)
    for piece in pieces[1:]:
        projected += piece[...].astype(f32)
    gate = modulation_ref[0, 0:1, :]
    shift = modulation_ref[0, 1:2, :]
    scale = modulation_ref[0, 2:3, :]
    residual = stream_ref[0].astype(f32) + gate * projected
    normed = (layer_norm(residual) * (1.0 + scale) + shift).astype(bf16)
    out_ref[...] = jnp.dot(normed, weight_ref[...], preferred_element_type=f32) + bias_ref[...]


def predict(stream, modulation, weight, bias, pieces):
    return pl.pallas_call(
        predict_kernel,
        out_shape=jax.ShapeDtypeStruct((stream.shape[1], weight.shape[1]), f32),
        compiler_params=params(),
        name="predict",
    )(stream, modulation, weight, bias, *pieces)


def next_projection_kernel(
    place_ref, patch_ref, position_ref, modulation_ref, weight_ref, gains_ref, *refs
):
    lows, out_ref, latents, inputs = refs[:-3], refs[-3], refs[-2], refs[-1]
    kind = pl.program_id(0)

    @pl.when(kind == 0)
    def _():
        count = len(lows)
        size = lows[0].shape[0]
        for step, low_ref in enumerate(lows):
            start = pl.multiple_of(lax.rem(place_ref[0] + count - step, count) * size, size)
            latents[pl.ds(start, size), :] = low_ref[...].astype(f32)
        embedded = jnp.dot(
            latents[...].astype(bf16), patch_ref[...], preferred_element_type=f32
        ) + position_ref[...].astype(f32)
        shift = modulation_ref[0, 3:4, :]
        scale = modulation_ref[0, 4:5, :]
        inputs[...] = (layer_norm(embedded) * (1.0 + scale) + shift).astype(bf16)

    product = jnp.dot(inputs[...], weight_ref[...], preferred_element_type=f32)

    @pl.when(kind < 2)
    def _():
        gain = jnp.where(kind == 0, gains_ref[0:1, :], gains_ref[1:2, :])
        low = low_lanes((product.shape[0], 128))
        for pair in range(product.shape[1] // 128):
            lanes = slice(128 * pair, 128 * pair + 128)
            block = product[:, lanes]
            squares = block * block
            left = jnp.sum(jnp.where(low, squares, 0.0), axis=-1, keepdims=True)
            right = jnp.sum(jnp.where(low, 0.0, squares), axis=-1, keepdims=True)
            mean = jnp.where(low, left, right) * (1.0 / HD)
            out_ref[0, 0, :, lanes] = (block * lax.rsqrt(mean + norm_epsilon) * gain).astype(bf16)

    @pl.when(kind == 2)
    def _():
        out_ref[0, 0] = product.astype(bf16)


def next_projection(place, lows, patch_weight, position, modulation, weight, gains):
    tokens, depth = position.shape
    columns = weight.shape[1] // 3
    return pl.pallas_call(
        next_projection_kernel,
        grid_spec=pltpu.PrefetchScalarGridSpec(
            num_scalar_prefetch=1,
            grid=(3,),
            in_specs=[
                whole(patch_weight.shape),
                whole(position.shape),
                whole(modulation.shape),
                pl.BlockSpec((depth, columns), lambda i, place: (0, i)),
                whole(gains.shape),
            ]
            + [whole(low.shape) for low in lows],
            out_specs=pl.BlockSpec((1, 1, tokens, columns), lambda i, place: (0, i, 0, 0)),
            scratch_shapes=[
                pltpu.VMEM((tokens, lows[0].shape[1]), f32),
                pltpu.VMEM((tokens, depth), bf16),
            ],
        ),
        out_shape=jax.ShapeDtypeStruct((1, 3, tokens, columns), bf16),
        compiler_params=params(),
        name="next_projection",
    )(place, patch_weight, position, modulation, weight, gains, *lows)


def turned(block, axis, step):
    count = lax.axis_size(axis)
    return lax.ppermute(block, axis, [(i, (i + step) % count) for i in range(count)])


def both_sides(block):
    other = turned(block, "yh", 1)
    first = lax.axis_index("yh") == 0
    return jnp.stack([jnp.where(first, block, other), jnp.where(first, other, block)])


def local(
    query,
    key,
    value,
    text_key,
    text_value,
    stream,
    modulation,
    out_weight,
    final_weight,
    final_bias,
    latents,
    sigmas,
    step_index,
    patch_weight,
    position,
    qkv_weight,
    norm_gains,
):
    zs, us = lax.axis_size("z"), lax.axis_size("uly")
    z, u = lax.axis_index("z"), lax.axis_index("uly")
    place = u.astype(jnp.int32).reshape(1)
    head = (zs * u + z).astype(jnp.int32).reshape(1)

    with jax.named_scope("weights"):
        out_gathered = lax.all_gather(both_sides(out_weight), ("z", "core"), axis=0)
        kinds, slab, columns = qkv_weight.shape
        flat_weight = qkv_weight.transpose(1, 0, 2).reshape(slab, kinds * columns)
        qkv_gathered = lax.all_gather(both_sides(flat_weight), ("z", "core"), axis=0)
        qkv_full = qkv_gathered.transpose(1, 0, 2, 3).reshape(-1, kinds * columns)

    with jax.named_scope("attention"):
        send, text = pack(zs, us, head, query, key, value, text_key, text_value)
        pieces = lax.all_to_all(send, ("z", "uly"), split_axis=0, concat_axis=0, tiled=True)
        rows = query.shape[1]
        own = pieces[:, :rows, :].reshape(zs * us * rows, 128)
        across = turned(own, "yh", 1)
        beside = turned(own, "core", 1)
        queries, peak, mixed = first_attend(text_key.shape[1], pieces, text, own)
        diagonal = turned(across, "core", 1)
        peak, mixed = next_attend(queries, peak, mixed, beside)
        sent = last_attend(zs, queries, peak, mixed, across, diagonal)
        attended = lax.all_to_all(sent, "z", split_axis=0, concat_axis=0, tiled=True)

    with jax.named_scope("prediction"):
        pieces = project(us, place, attended, out_gathered)
        pieces = [pieces[0]] + [turned(pieces[step], "uly", step) for step in range(1, us)]
        predicted = predict(stream, modulation, final_weight, final_bias.reshape(1, -1), pieces)
        partner = turned(predicted, "cfg", 1)
        is_first = lax.axis_index("cfg") == 0
        with_text = jnp.where(is_first, predicted, partner)
        without_text = jnp.where(is_first, partner, predicted)
        velocity = without_text + guidance_scale * (with_text - without_text)
        moment = step_index[0]
        latents_next = latents + (sigmas[moment + 1] - sigmas[moment]) * velocity
        latents_low = latents_next.astype(bf16)

    with jax.named_scope("next"):
        lows = [latents_low] + [turned(latents_low, "uly", step) for step in range(1, us)]
        gains = jnp.concatenate([norm_gains, norm_gains], axis=1)
        next_qkv = next_projection(place, lows, patch_weight, position, modulation, qkv_full, gains)
    return (velocity, latents_next, next_qkv)


def solution(mesh):
    sizes = dict(mesh.shape)
    fine = Mesh(
        mesh.devices.reshape(sizes["cfg"], 2, sizes["blk"] // 4, 2, sizes["uly"]),
        ("cfg", "yh", "z", "core", "uly"),
    )
    blk = ("yh", "z", "core")
    tokens = blk + ("uly",)
    placed = (
        P("cfg", tokens, None),
        P("cfg", tokens, None),
        P("cfg", tokens, None),
        P("cfg", None, None),
        P("cfg", None, None),
        P("cfg", tokens, None),
        P("cfg", None, None),
        P(("uly",) + blk, None),
        P(),
        P(),
        P(tokens, None),
        P(),
        P(),
        P(),
        P(blk, None),
        P(None, blk, "uly"),
        P(),
    )
    return jax.shard_map(
        local,
        mesh=fine,
        in_specs=placed,
        out_specs=(P(tokens, None), P(tokens, None), P("cfg", None, blk, "uly")),
        check_vma=False,
    )
```

```python
import functools

import jax
import jax.numpy as jnp
from jax import lax
from jax.experimental import pallas as pl
from jax.experimental.pallas import tpu as pltpu
from jax.sharding import Mesh, PartitionSpec as P

HD = 64
norm_epsilon = 1e-06
guidance_scale = 3.5
bf16 = jnp.bfloat16
f32 = jnp.float32
KEY_BLOCK = 1024


def params(limit_mib=56, **more):
    return pltpu.CompilerParams(vmem_limit_bytes=limit_mib * 2**20, **more)


def whole(shape):
    return pl.BlockSpec(shape, lambda *_: (0,) * len(shape))


def half_swap(block):
    return pltpu.roll(block.astype(f32), 64, 1).astype(block.dtype)


def low_lanes(shape):
    return lax.broadcasted_iota(jnp.int32, shape, len(shape) - 1) < 64


def pack_kernel(zs, us, head_ref, query_ref, key_ref, value_ref, text_key_ref, text_value_ref, send_ref, text_ref):
    rows = query_ref.shape[1]
    half = rows // 2
    low = low_lanes((rows, 128))
    low_half = low_lanes((half, 128))
    for pair in range(zs * us // 2):
        lanes = slice(128 * pair, 128 * pair + 128)
        keys = key_ref[0, :, lanes]
        values = value_ref[0, :, lanes]
        queries = query_ref[0, :, lanes] * 0.125
        first, second = queries[:half], queries[half:]
        for odd in range(2):
            head = 2 * pair + odd
            place = (head % zs) * us + head // zs
            if odd:
                both = jnp.where(low, half_swap(keys), values)
                folded = jnp.where(low_half, half_swap(first), second)
            else:
                both = jnp.where(low, keys, half_swap(values))
                folded = jnp.where(low_half, first, half_swap(second))
            send_ref[place, :rows, :] = both
            send_ref[place, rows:, :] = folded
    odd_head = lax.rem(head_ref[0], 2) == 1
    text_rows = text_key_ref.shape[1]
    text_low = low_lanes((text_rows, 128))
    keys = text_key_ref[0]
    values = text_value_ref[0]
    both = jnp.where(
        text_low,
        jnp.where(odd_head, half_swap(keys), keys),
        jnp.where(odd_head, values, half_swap(values)),
    )
    text_ref[...] = jnp.zeros(text_ref.shape, bf16)
    text_ref[:text_rows, :] = both


def pack(zs, us, head, query, key, value, text_key, text_value):
    rows = query.shape[1]
    text_rows = text_key.shape[1]
    text_padded = -(-text_rows // 128) * 128
    text_spec = pl.BlockSpec((1, text_rows, 128), lambda i, head: (0, 0, head[0] // 2))
    return pl.pallas_call(
        functools.partial(pack_kernel, zs, us),
        grid_spec=pltpu.PrefetchScalarGridSpec(
            num_scalar_prefetch=1,
            grid=(1,),
            in_specs=[whole(query.shape), whole(key.shape), whole(value.shape), text_spec, text_spec],
            out_specs=[whole((zs * us, rows + rows // 2, 128)), whole((text_padded, 128))],
        ),
        out_shape=[
            jax.ShapeDtypeStruct((zs * us, rows + rows // 2, 128), bf16),
            jax.ShapeDtypeStruct((text_padded, 128), bf16),
        ],
        compiler_params=params(),
        name="pack",
    )(head, query, key, value, text_key, text_value)


def value_rows(both):
    return jnp.concatenate([jnp.transpose(both)[64:], jnp.ones((16, both.shape[0]), bf16)], axis=0)


def scores_of(both, queries):
    return lax.dot_general(both, queries, (((1,), (1,)), ((), ())), preferred_element_type=f32)


def fold(peak, mixed, both, queries):
    scores = scores_of(both, queries)
    new_peak = jnp.maximum(peak, jnp.max(scores, axis=0, keepdims=True))
    weights = jnp.exp(scores - new_peak).astype(bf16)
    mixed = mixed * jnp.exp(peak - new_peak) + jnp.dot(value_rows(both), weights, preferred_element_type=f32)
    return new_peak, mixed


def fold_all(peak, mixed, both_refs, queries):
    for both_ref in both_refs:
        for start in range(0, both_ref.shape[0], KEY_BLOCK):
            peak, mixed = fold(peak, mixed, both_ref[start : start + KEY_BLOCK, :], queries)
    return peak, mixed


def first_kernel(text_count, pieces_ref, text_ref, own_ref, beside_ref, queries_ref, peak_ref, mixed_ref):
    count, height, _ = pieces_ref.shape
    half = height // 3
    folded = pieces_ref[:, 2 * half :, :].reshape(count * half, 128)
    low = low_lanes(folded.shape)
    zero = jnp.zeros_like(folded)
    first = jnp.where(low, folded, zero).reshape(count, half, 128)
    second = jnp.where(low, half_swap(folded), zero).reshape(count, half, 128)
    queries = jnp.concatenate([first, second], axis=1).reshape(count * 2 * half, 128)
    queries_ref[...] = queries
    text = text_ref[...]
    scores = scores_of(text, queries)
    kept = lax.broadcasted_iota(jnp.int32, scores.shape, 0) < text_count
    scores = jnp.where(kept, scores, -1e30)
    peak = jnp.max(scores, axis=0, keepdims=True)
    weights = jnp.exp(scores - peak).astype(bf16)
    mixed = jnp.dot(value_rows(text), weights, preferred_element_type=f32)
    peak_ref[...], mixed_ref[...] = fold_all(peak, mixed, (own_ref, beside_ref), queries)


def first_attend(text_count, pieces, text, own, beside):
    count, height, _ = pieces.shape
    total = count * (height // 3) * 2
    return pl.pallas_call(
        functools.partial(first_kernel, text_count),
        out_shape=[
            jax.ShapeDtypeStruct((total, 128), bf16),
            jax.ShapeDtypeStruct((1, total), f32),
            jax.ShapeDtypeStruct((80, total), f32),
        ],
        compiler_params=params(),
        name="attend_first",
    )(pieces, text, own, beside)


def last_kernel(queries_ref, peak_ref, mixed_ref, across_ref, diagonal_ref, out_ref):
    _, mixed = fold_all(peak_ref[...], mixed_ref[...], (across_ref, diagonal_ref), queries_ref[...])
    attended = (mixed[:64] / mixed[64:65]).astype(bf16)
    width = out_ref.shape[2]
    for place in range(out_ref.shape[0]):
        out_ref[place] = attended[:, place * width : place * width + width]


def last_attend(zs, queries, peak, mixed, across, diagonal):
    return pl.pallas_call(
        last_kernel,
        out_shape=jax.ShapeDtypeStruct((zs, 64, queries.shape[0] // zs), bf16),
        compiler_params=params(),
        name="attend_last",
    )(queries, peak, mixed, across, diagonal)


def project_kernel(place_ref, attended_ref, near_ref, mine_ref, theirs_ref, *refs):
    outs, held = refs[:-1], refs[-1]
    heads, _, tokens = attended_ref.shape
    side, core = place_ref[1], place_ref[2]

    def term(first, count, weight_ref):
        rows = attended_ref[pl.ds(first, count)].reshape(count * 64, tokens)
        return jnp.dot(jnp.transpose(rows), weight_ref[...], preferred_element_type=f32)

    far = (1 - side) * (heads // 2)
    total = term(side * (heads // 2), heads // 2, near_ref)
    total += term(far + core * (heads // 4), heads // 4, mine_ref)
    total += term(far + (1 - core) * (heads // 4), heads // 4, theirs_ref)
    held[...] = total.astype(bf16)
    count = len(outs)
    size = tokens // count
    for step, out_ref in enumerate(outs):
        start = pl.multiple_of(lax.rem(place_ref[0] + step, count) * size, size)
        out_ref[...] = held[pl.ds(start, size), :]


def project(us, place, attended, near, mine, theirs):
    tokens = attended.shape[2]
    width = near.shape[-1]
    piece = (tokens // us, width)
    return pl.pallas_call(
        project_kernel,
        grid_spec=pltpu.PrefetchScalarGridSpec(
            num_scalar_prefetch=1,
            grid=(1,),
            in_specs=[whole(attended.shape), whole(near.shape), whole(mine.shape), whole(theirs.shape)],
            out_specs=[whole(piece)] * us,
            scratch_shapes=[pltpu.VMEM((tokens, width), bf16)],
        ),
        out_shape=[jax.ShapeDtypeStruct(piece, bf16)] * us,
        compiler_params=params(),
        name="project",
    )(place, attended, near, mine, theirs)


def layer_norm(matrix):
    mean = jnp.mean(matrix, axis=-1, keepdims=True)
    centred = matrix - mean
    variance = jnp.mean(centred * centred, axis=-1, keepdims=True)
    return centred * lax.rsqrt(variance + norm_epsilon)


def predict_kernel(stream_ref, modulation_ref, weight_ref, bias_ref, *refs):
    pieces, out_ref = refs[:-1], refs[-1]
    projected = pieces[0][...].astype(f32)
    for piece in pieces[1:]:
        projected += piece[...].astype(f32)
    gate = modulation_ref[0, 0:1, :]
    shift = modulation_ref[0, 1:2, :]
    scale = modulation_ref[0, 2:3, :]
    residual = stream_ref[0].astype(f32) + gate * projected
    normed = (layer_norm(residual) * (1.0 + scale) + shift).astype(bf16)
    out_ref[...] = jnp.dot(normed, weight_ref[...], preferred_element_type=f32) + bias_ref[...]


def predict(stream, modulation, weight, bias, pieces):
    return pl.pallas_call(
        predict_kernel,
        out_shape=jax.ShapeDtypeStruct((stream.shape[1], weight.shape[1]), f32),
        compiler_params=params(),
        name="predict",
    )(stream, modulation, weight, bias, *pieces)


def euler_kernel(step_ref, sigmas_ref, own_ref, partner_ref, latents_ref, velocity_ref, next_ref, low_ref):
    own, partner = own_ref[...], partner_ref[...]
    first = step_ref[1] == 0
    with_text = jnp.where(first, own, partner)
    without_text = jnp.where(first, partner, own)
    velocity = without_text + guidance_scale * (with_text - without_text)
    moment = step_ref[0]
    moved = latents_ref[...] + (sigmas_ref[moment + 1] - sigmas_ref[moment]) * velocity
    velocity_ref[...] = velocity
    next_ref[...] = moved
    low_ref[...] = moved.astype(bf16)


def euler(step, sigmas, own, partner, latents):
    scalars = pl.BlockSpec(memory_space=pltpu.SMEM)
    block = pl.BlockSpec(memory_space=pltpu.VMEM)
    return pl.pallas_call(
        euler_kernel,
        in_specs=[scalars, scalars, block, block, block],
        out_specs=[block] * 3,
        out_shape=[jax.ShapeDtypeStruct(own.shape, kind) for kind in (f32, f32, bf16)],
        compiler_params=params(),
        name="euler",
    )(step, sigmas, own, partner, latents)


def next_projection_kernel(
    place_ref, patch_ref, position_ref, modulation_ref, weight_ref, gains_ref, *refs
):
    lows, out_ref, latents, inputs = refs[:-3], refs[-3], refs[-2], refs[-1]
    kind = pl.program_id(0)

    @pl.when(kind == 0)
    def _():
        count = len(lows)
        size = lows[0].shape[0]
        for step, low_ref in enumerate(lows):
            start = pl.multiple_of(lax.rem(place_ref[0] + count - step, count) * size, size)
            latents[pl.ds(start, size), :] = low_ref[...].astype(f32)
        embedded = jnp.dot(
            latents[...].astype(bf16), patch_ref[...], preferred_element_type=f32
        ) + position_ref[...].astype(f32)
        shift = modulation_ref[0, 3:4, :]
        scale = modulation_ref[0, 4:5, :]
        inputs[...] = (layer_norm(embedded) * (1.0 + scale) + shift).astype(bf16)

    product = jnp.dot(inputs[...], weight_ref[...], preferred_element_type=f32)

    @pl.when(kind < 2)
    def _():
        gain = jnp.where(kind == 0, gains_ref[0:1, :], gains_ref[1:2, :])
        low = low_lanes((product.shape[0], 128))
        for pair in range(product.shape[1] // 128):
            lanes = slice(128 * pair, 128 * pair + 128)
            block = product[:, lanes]
            squares = block * block
            left = jnp.sum(jnp.where(low, squares, 0.0), axis=-1, keepdims=True)
            right = jnp.sum(jnp.where(low, 0.0, squares), axis=-1, keepdims=True)
            mean = jnp.where(low, left, right) * (1.0 / HD)
            out_ref[0, 0, :, lanes] = (block * lax.rsqrt(mean + norm_epsilon) * gain).astype(bf16)

    @pl.when(kind == 2)
    def _():
        out_ref[0, 0] = product.astype(bf16)


def next_projection(place, lows, patch_weight, position, modulation, weight, gains):
    tokens, depth = position.shape
    columns = weight.shape[1] // 3
    return pl.pallas_call(
        next_projection_kernel,
        grid_spec=pltpu.PrefetchScalarGridSpec(
            num_scalar_prefetch=1,
            grid=(3,),
            in_specs=[
                whole(patch_weight.shape),
                whole(position.shape),
                whole(modulation.shape),
                pl.BlockSpec((depth, columns), lambda i, place: (0, i)),
                whole(gains.shape),
            ]
            + [whole(low.shape) for low in lows],
            out_specs=pl.BlockSpec((1, 1, tokens, columns), lambda i, place: (0, i, 0, 0)),
            scratch_shapes=[
                pltpu.VMEM((tokens, lows[0].shape[1]), f32),
                pltpu.VMEM((tokens, depth), bf16),
            ],
        ),
        out_shape=jax.ShapeDtypeStruct((1, 3, tokens, columns), bf16),
        compiler_params=params(),
        name="next_projection",
    )(place, patch_weight, position, modulation, weight, gains, *lows)


def turned(block, axis, step):
    count = lax.axis_size(axis)
    return lax.ppermute(block, axis, [(i, (i + step) % count) for i in range(count)])


def after(value, *others):
    return lax.optimization_barrier((value, others))[0]


def gathered_order(matrix, sides, slab):
    lead, depth = matrix.shape[:-1], matrix.shape[-1]
    split = matrix.reshape(lead + (sides, depth // (sides * slab), slab))
    return jnp.swapaxes(split, -3, -2).reshape(lead + (depth,))


def local(
    query,
    key,
    value,
    text_key,
    text_value,
    stream,
    modulation,
    out_weight,
    final_weight,
    final_bias,
    latents,
    sigmas,
    step_index,
    patch_weight,
    position,
    qkv_weight,
    norm_gains,
):
    zs, us = lax.axis_size("z"), lax.axis_size("uly")
    z, u = lax.axis_index("z"), lax.axis_index("uly")
    side, core = lax.axis_index("yh"), lax.axis_index("core")
    place = jnp.stack([u, side, core]).astype(jnp.int32)
    head = (zs * u + z).astype(jnp.int32).reshape(1)
    rows = query.shape[1]
    kinds, slab, columns = qkv_weight.shape

    near = lax.all_gather(out_weight, ("z", "core"), axis=0, tiled=True)
    flat = qkv_weight.transpose(1, 0, 2).reshape(slab, kinds * columns)
    flat_other = turned(flat, "yh", 1)
    send, text = pack(zs, us, head, query, key, value, text_key, text_value)
    pieces = lax.all_to_all(send, ("z", "uly"), split_axis=0, concat_axis=0, tiled=True)

    own = pieces[:, :rows, :].reshape(zs * us * rows, 128)
    beside = turned(own, "core", 1)
    across = turned(own, "yh", 1)

    flat_other = after(flat_other, pieces)
    is_low = side == 0
    stacked = jnp.concatenate([jnp.where(is_low, flat, flat_other), jnp.where(is_low, flat_other, flat)])
    qkv_full = lax.all_gather(stacked, ("z", "core"), axis=0, tiled=True)

    queries, peak, mixed = first_attend(text_key.shape[1], pieces, text, own, beside)
    across, near, patch = after((across, near, patch_weight), peak)
    mine = turned(lax.dynamic_slice_in_dim(near, core * (near.shape[0] // 2), near.shape[0] // 2, 0), "yh", 1)
    diagonal = turned(across, "core", 1)
    patch = gathered_order(patch, 2, slab)
    queries = after(queries, patch)
    sent = last_attend(zs, queries, peak, mixed, across, diagonal)
    mine = after(mine, sent)
    theirs = turned(mine, "core", 1)
    attended = lax.all_to_all(sent, "z", split_axis=0, concat_axis=0, tiled=True)

    pieces = project(us, place, attended, near, mine, theirs)
    others = [turned(pieces[step], "uly", step) for step in range(1, us)]
    spots, shifts = after((position, modulation), pieces[0])
    spots = gathered_order(spots, 2, slab)
    shifts = gathered_order(shifts, 2, slab)
    others = after(others, spots, shifts)
    predicted = predict(stream, modulation, final_weight, final_bias.reshape(1, -1), [pieces[0]] + others)
    partner = turned(predicted, "cfg", 1)
    step = jnp.stack([step_index[0], lax.axis_index("cfg").astype(jnp.int32)])
    velocity, latents_next, latents_low = euler(step, sigmas, predicted, partner, latents)

    lows = [latents_low] + [turned(latents_low, "uly", step) for step in range(1, us)]
    gains = jnp.concatenate([norm_gains, norm_gains], axis=1)
    next_qkv = next_projection(place, lows, patch, spots, shifts, qkv_full, gains)
    return (velocity, latents_next, next_qkv)


def solution(mesh):
    sizes = dict(mesh.shape)
    fine = Mesh(
        mesh.devices.reshape(sizes["cfg"], 2, sizes["blk"] // 4, 2, sizes["uly"]),
        ("cfg", "yh", "z", "core", "uly"),
    )
    blk = ("yh", "z", "core")
    tokens = blk + ("uly",)
    placed = (
        P("cfg", tokens, None),
        P("cfg", tokens, None),
        P("cfg", tokens, None),
        P("cfg", None, None),
        P("cfg", None, None),
        P("cfg", tokens, None),
        P("cfg", None, None),
        P(("uly",) + blk, None),
        P(),
        P(),
        P(tokens, None),
        P(),
        P(),
        P(),
        P(blk, None),
        P(None, blk, "uly"),
        P(),
    )
    return jax.shard_map(
        local,
        mesh=fine,
        in_specs=placed,
        out_specs=(P(tokens, None), P(tokens, None), P("cfg", None, blk, "uly")),
        check_vma=False,
    )
```

```python
import functools

import jax
import jax.numpy as jnp
from jax import lax
from jax.experimental import pallas as pl
from jax.experimental.pallas import tpu as pltpu
from jax.sharding import Mesh, PartitionSpec as P

HD = 64
norm_epsilon = 1e-06
guidance_scale = 3.5
bf16 = jnp.bfloat16
f32 = jnp.float32
KEY_BLOCK = 1024
WEIGHT_PARTS = 5
SOURCE_PARTS = 4


def params(limit_mib, **more):
    return pltpu.CompilerParams(vmem_limit_bytes=limit_mib * 2**20, **more)


def attention_cost(queries, keys):
    return pl.CostEstimate(
        flops=queries * keys * 1024, transcendentals=queries * keys, bytes_accessed=(queries + keys) * 512
    )


def whole(shape):
    return pl.BlockSpec(shape, lambda *_: (0,) * len(shape))


def half_swap(block):
    return pltpu.roll(block.astype(f32), 64, 1).astype(block.dtype)


def low_lanes(shape):
    return lax.broadcasted_iota(jnp.int32, shape, len(shape) - 1) < 64


def pack_kernel(zs, us, head_ref, query_ref, key_ref, value_ref, text_key_ref, text_value_ref, send_ref, text_ref):
    rows = query_ref.shape[1]
    half = rows // 2
    low = low_lanes((rows, 128))
    low_half = low_lanes((half, 128))
    for pair in range(zs * us // 2):
        lanes = slice(128 * pair, 128 * pair + 128)
        keys = key_ref[0, :, lanes]
        values = value_ref[0, :, lanes]
        queries = query_ref[0, :, lanes] * 0.125
        first, second = queries[:half], queries[half:]
        for odd in range(2):
            head = 2 * pair + odd
            place = (head % zs) * us + head // zs
            if odd:
                both = jnp.where(low, half_swap(keys), values)
                folded = jnp.where(low_half, half_swap(first), second)
            else:
                both = jnp.where(low, keys, half_swap(values))
                folded = jnp.where(low_half, first, half_swap(second))
            send_ref[place, :rows, :] = both
            send_ref[place, rows:, :] = folded
    odd_head = lax.rem(head_ref[0], 2) == 1
    text_rows = text_key_ref.shape[1]
    text_low = low_lanes((text_rows, 128))
    keys = text_key_ref[0]
    values = text_value_ref[0]
    both = jnp.where(
        text_low,
        jnp.where(odd_head, half_swap(keys), keys),
        jnp.where(odd_head, values, half_swap(values)),
    )
    text_ref[...] = jnp.zeros(text_ref.shape, bf16)
    text_ref[:text_rows, :] = both


def pack(zs, us, head, query, key, value, text_key, text_value):
    rows = query.shape[1]
    text_rows = text_key.shape[1]
    text_padded = -(-text_rows // 128) * 128
    text_spec = pl.BlockSpec((1, text_rows, 128), lambda i, head: (0, 0, head[0] // 2))
    return pl.pallas_call(
        functools.partial(pack_kernel, zs, us),
        grid_spec=pltpu.PrefetchScalarGridSpec(
            num_scalar_prefetch=1,
            grid=(1,),
            in_specs=[whole(query.shape), whole(key.shape), whole(value.shape), text_spec, text_spec],
            out_specs=[whole((zs * us, rows + rows // 2, 128)), whole((text_padded, 128))],
        ),
        out_shape=[
            jax.ShapeDtypeStruct((zs * us, rows + rows // 2, 128), bf16),
            jax.ShapeDtypeStruct((text_padded, 128), bf16),
        ],
        compiler_params=params(56),
        name="pack",
    )(head, query, key, value, text_key, text_value)


def values_and_ones(both):
    return jnp.where(low_lanes(both.shape), jnp.ones_like(both), both)


def weighted(both, weights):
    return lax.dot_general(
        values_and_ones(both), weights, (((0,), (0,)), ((), ())), preferred_element_type=f32
    )


def scores_of(both, queries):
    return lax.dot_general(both, queries, (((1,), (1,)), ((), ())), preferred_element_type=f32)


def fold(peak, mixed, both, queries):
    scores = scores_of(both, queries)
    new_peak = jnp.maximum(peak, jnp.max(scores, axis=0, keepdims=True))
    weights = jnp.exp(scores - new_peak).astype(bf16)
    mixed = mixed * jnp.exp(peak - new_peak) + weighted(both, weights)
    return new_peak, mixed


def fold_all(peak, mixed, both_refs, queries):
    for both_ref in both_refs:
        for start in range(0, both_ref.shape[0], KEY_BLOCK):
            peak, mixed = fold(peak, mixed, both_ref[start : start + KEY_BLOCK, :], queries)
    return peak, mixed


def first_kernel(text_count, pieces_ref, text_ref, own_ref, beside_ref, queries_ref, peak_ref, mixed_ref):
    count, height, _ = pieces_ref.shape
    half = height // 3
    folded = pieces_ref[:, 2 * half :, :].reshape(count * half, 128)
    low = low_lanes(folded.shape)
    zero = jnp.zeros_like(folded)
    first = jnp.where(low, folded, zero).reshape(count, half, 128)
    second = jnp.where(low, half_swap(folded), zero).reshape(count, half, 128)
    queries = jnp.concatenate([first, second], axis=1).reshape(count * 2 * half, 128)
    queries_ref[...] = queries
    text = text_ref[...]
    scores = scores_of(text, queries)
    kept = lax.broadcasted_iota(jnp.int32, scores.shape, 0) < text_count
    scores = jnp.where(kept, scores, -1e30)
    peak = jnp.max(scores, axis=0, keepdims=True)
    weights = jnp.exp(scores - peak).astype(bf16)
    mixed = weighted(text, weights)
    peak_ref[...], mixed_ref[...] = fold_all(peak, mixed, (own_ref, beside_ref), queries)


def first_attend(text_count, pieces, text, own, beside):
    count, height, _ = pieces.shape
    total = count * (height // 3) * 2
    return pl.pallas_call(
        functools.partial(first_kernel, text_count),
        out_shape=[
            jax.ShapeDtypeStruct((total, 128), bf16),
            jax.ShapeDtypeStruct((1, total), f32),
            jax.ShapeDtypeStruct((128, total), f32),
        ],
        compiler_params=params(56),
        cost_estimate=attention_cost(total, text.shape[0] + own.shape[0] + beside.shape[0]),
        name="attend_first",
    )(pieces, text, own, beside)


def last_kernel(queries_ref, peak_ref, mixed_ref, across_ref, diagonal_ref, out_ref):
    _, mixed = fold_all(peak_ref[...], mixed_ref[...], (across_ref, diagonal_ref), queries_ref[...])
    attended = (mixed[64:] / mixed[0:1]).astype(bf16)
    width = out_ref.shape[2]
    for place in range(out_ref.shape[0]):
        out_ref[place] = attended[:, place * width : place * width + width]


def last_attend(zs, queries, peak, mixed, across, diagonal):
    total = queries.shape[0]
    return pl.pallas_call(
        last_kernel,
        out_shape=jax.ShapeDtypeStruct((zs, 64, total // zs), bf16),
        compiler_params=params(56),
        cost_estimate=attention_cost(total, across.shape[0] + diagonal.shape[0]),
        name="attend_last",
    )(queries, peak, mixed, across, diagonal)


def bundle_kernel(side_ref, out_ref, out_other_ref, next_ref, next_other_ref, first_ref, second_ref):
    low = side_ref[0] == 0

    def pair(own, other):
        return jnp.where(low, own, other), jnp.where(low, other, own)

    rows, width = out_ref.shape
    sets = -(-width // 256)
    for index in range(sets):
        lanes = slice(256 * index, min(256 * index + 256, width))
        count = lanes.stop - lanes.start
        for place, block in enumerate(pair(out_ref[:, lanes], out_other_ref[:, lanes])):
            start = (2 * index + place) * rows
            if count < 256:
                first_ref[start : start + rows, :] = jnp.zeros((rows, 256), bf16)
            first_ref[start : start + rows, :count] = block
    kinds, slab, _ = next_ref.shape
    padded = padded_rows(2 * slab)
    for half, target in enumerate((first_ref, second_ref)):
        base = target.shape[0] - kinds * padded
        lanes = slice(256 * half, 256 * half + 256)
        for kind in range(kinds):
            start = base + kind * padded
            target[start : start + padded, :] = jnp.zeros((padded, 256), bf16)
            for place, block in enumerate(pair(next_ref[kind, :, lanes], next_other_ref[kind, :, lanes])):
                target[start + place * slab : start + place * slab + slab, :] = block


def padded_rows(rows):
    return -(-rows // 16) * 16


def bundle(place, out_weight, out_other, next_weight, next_other):
    rows, width = out_weight.shape
    kinds, slab, columns = next_weight.shape
    second = kinds * padded_rows(2 * slab)
    first = 2 * rows * -(-width // 256) + second
    block = pl.BlockSpec(memory_space=pltpu.VMEM)
    return pl.pallas_call(
        bundle_kernel,
        in_specs=[pl.BlockSpec(memory_space=pltpu.SMEM)] + [block] * 4,
        out_specs=[block] * 2,
        out_shape=[jax.ShapeDtypeStruct((count, columns // 2), bf16) for count in (first, second)],
        compiler_params=params(8),
        name="bundle",
    )(place, out_weight, out_other, next_weight, next_other)


def project_kernel(place_ref, attended_ref, *refs):
    weights, outs, held = refs[:WEIGHT_PARTS], refs[WEIGHT_PARTS:-1], refs[-1]
    heads, _, tokens = attended_ref.shape
    sources, rows, _ = weights[0].shape
    slab = heads * 64 // (2 * sources)
    blocks = attended_ref[...].reshape(2, sources, slab, tokens)
    attended = jnp.concatenate([blocks[side, source] for source in range(sources) for side in range(2)], axis=0)
    attended = jnp.transpose(attended)
    width = held.shape[1]
    sets = rows // (2 * slab)
    for index in range(WEIGHT_PARTS * sets):
        start = index % sets * 2 * slab
        part = weights[index // sets][:, start : start + 2 * slab, :].reshape(heads * 64, 256)
        lanes = slice(256 * index, min(256 * index + 256, width))
        count = lanes.stop - lanes.start
        held[:, lanes] = jnp.dot(attended, part[:, :count], preferred_element_type=f32).astype(bf16)
    count = len(outs)
    size = tokens // count
    for order, out_ref in enumerate(outs):
        start = pl.multiple_of(lax.rem(place_ref[0] + order, count) * size, size)
        out_ref[...] = held[pl.ds(start, size), :]


def project(us, width, place, attended, bundles, base):
    tokens = attended.shape[2]
    piece = (tokens // us, width)
    part = (bundles.shape[0], base // WEIGHT_PARTS, 256)
    return pl.pallas_call(
        project_kernel,
        grid_spec=pltpu.PrefetchScalarGridSpec(
            num_scalar_prefetch=1,
            grid=(1,),
            in_specs=[whole(attended.shape)]
            + [pl.BlockSpec(part, functools.partial(lambda at, i, place: (0, at, 0), at)) for at in range(WEIGHT_PARTS)],
            out_specs=[whole(piece)] * us,
            scratch_shapes=[pltpu.VMEM((tokens, width), bf16)],
        ),
        out_shape=[jax.ShapeDtypeStruct(piece, bf16)] * us,
        compiler_params=params(56),
        name="project",
    )(place, attended, *[bundles] * WEIGHT_PARTS)


def layer_norm(matrix):
    mean = jnp.mean(matrix, axis=-1, keepdims=True)
    centred = matrix - mean
    variance = jnp.mean(centred * centred, axis=-1, keepdims=True)
    return centred * lax.rsqrt(variance + norm_epsilon)


def predict_kernel(parts, held, stream_ref, modulation_ref, weight_ref, bias_ref, *refs):
    pieces, out_ref = refs[: len(refs) - 1 - held], refs[-1]
    count = len(pieces) // parts
    gate = modulation_ref[0, 0:1, :]
    shift = modulation_ref[0, 1:2, :]
    scale = modulation_ref[0, 2:3, :]
    size = out_ref.shape[0] // parts
    for part in range(parts):
        projected = pieces[part * count][...].astype(f32)
        for piece in pieces[part * count + 1 : part * count + count]:
            projected += piece[...].astype(f32)
        rows = slice(part * size, part * size + size)
        residual = stream_ref[0, rows, :].astype(f32) + gate * projected
        normed = (layer_norm(residual) * (1.0 + scale) + shift).astype(bf16)
        out_ref[rows, :] = jnp.dot(normed, weight_ref[...], preferred_element_type=f32) + bias_ref[...]


def predict(stream, modulation, weight, bias, parts, held):
    pieces = [piece for part in parts for piece in part]
    block = pl.BlockSpec(memory_space=pltpu.VMEM)
    return pl.pallas_call(
        functools.partial(predict_kernel, len(parts), len(held)),
        in_specs=[block] * (4 + len(pieces)) + [pl.BlockSpec(memory_space=pl.ANY)] * len(held),
        out_specs=block,
        out_shape=jax.ShapeDtypeStruct((stream.shape[1], weight.shape[1]), f32),
        compiler_params=params(12),
        name="predict",
    )(stream, modulation, weight, bias, *pieces, *held)


def euler_kernel(step_ref, sigmas_ref, own_ref, partner_ref, latents_ref, velocity_ref, next_ref, low_ref):
    own, partner = own_ref[...], partner_ref[...]
    first = step_ref[1] == 0
    with_text = jnp.where(first, own, partner)
    without_text = jnp.where(first, partner, own)
    velocity = without_text + guidance_scale * (with_text - without_text)
    moment = step_ref[0]
    moved = latents_ref[...] + (sigmas_ref[moment + 1] - sigmas_ref[moment]) * velocity
    velocity_ref[...] = velocity
    next_ref[...] = moved
    low_ref[...] = moved.astype(bf16)


def euler(step, sigmas, own, partner, latents):
    scalars = pl.BlockSpec(memory_space=pltpu.SMEM)
    block = pl.BlockSpec(memory_space=pltpu.VMEM)
    return pl.pallas_call(
        euler_kernel,
        in_specs=[scalars, scalars, block, block, block],
        out_specs=[block] * 3,
        out_shape=[jax.ShapeDtypeStruct(own.shape, kind) for kind in (f32, f32, bf16)],
        compiler_params=params(4),
        name="euler",
    )(step, sigmas, own, partner, latents)


def project_heads(kind, inputs_ref, weight_refs, gains_ref, out_ref):
    sources, rows, columns = weight_refs[0].shape
    depth = sources * rows
    product = jnp.zeros((inputs_ref.shape[0], columns), f32)
    for order, weight_ref in enumerate(weight_refs):
        part = inputs_ref[:, order * depth : order * depth + depth]
        product += jnp.dot(part, weight_ref[...].reshape(depth, columns), preferred_element_type=f32)

    @pl.when(kind < 2)
    def _():
        gain = jnp.where(kind == 0, gains_ref[0:1, :], gains_ref[1:2, :])
        low = low_lanes((product.shape[0], 128))
        for pair in range(columns // 128):
            lanes = slice(128 * pair, 128 * pair + 128)
            block = product[:, lanes]
            squares = block * block
            left = jnp.sum(jnp.where(low, squares, 0.0), axis=-1, keepdims=True)
            right = jnp.sum(jnp.where(low, 0.0, squares), axis=-1, keepdims=True)
            mean = jnp.where(low, left, right) * (1.0 / HD)
            out_ref[0, 0, :, lanes] = (block * lax.rsqrt(mean + norm_epsilon) * gain).astype(bf16)

    @pl.when(kind == 2)
    def _():
        out_ref[0, 0] = product.astype(bf16)


def embed_kernel(depth, place_ref, patch_ref, position_ref, rows_ref, gains_ref, *refs):
    weights, lows = refs[:SOURCE_PARTS], refs[SOURCE_PARTS:-3]
    out_ref, inputs, latents = refs[-3:]

    @pl.when(pl.program_id(0) == 0)
    def _():
        count = len(lows)
        size = lows[0].shape[0]
        for order, low_ref in enumerate(lows):
            start = pl.multiple_of(lax.rem(place_ref[0] + count - order, count) * size, size)
            latents[pl.ds(start, size), :] = low_ref[...].astype(f32)
        embedded = jnp.dot(
            latents[...].astype(bf16), patch_ref[...], preferred_element_type=f32
        ) + position_ref[...].astype(f32)
        mean = jnp.sum(embedded, axis=-1, keepdims=True) * (1.0 / depth)
        centred = (embedded - mean) * rows_ref[2:3, :]
        variance = jnp.sum(centred * centred, axis=-1, keepdims=True) * (1.0 / depth)
        base = centred * lax.rsqrt(variance + norm_epsilon)
        inputs[...] = (base * (1.0 + rows_ref[1:2, :]) + rows_ref[0:1, :]).astype(bf16)

    project_heads(pl.program_id(0), inputs, weights, gains_ref, out_ref)


def weight_blocks(weight, base):
    sources, total, columns = weight.shape
    each = (total - base) // 3
    shape = (sources // SOURCE_PARTS, each, columns)
    return [
        pl.BlockSpec(shape, functools.partial(lambda at, i, *_: (at, base // each + i, 0), at))
        for at in range(SOURCE_PARTS)
    ]


def embed(depth, place, lows, patch, position, rows, weight, base, gains):
    tokens, padded = position.shape
    columns = weight.shape[2]
    return pl.pallas_call(
        functools.partial(embed_kernel, depth),
        grid_spec=pltpu.PrefetchScalarGridSpec(
            num_scalar_prefetch=1,
            grid=(3,),
            in_specs=[whole(patch.shape), whole(position.shape), whole(rows.shape), whole(gains.shape)]
            + weight_blocks(weight, base)
            + [whole(low.shape) for low in lows],
            out_specs=[
                pl.BlockSpec((1, 1, tokens, columns), lambda i, place: (0, i, 0, 0)),
                whole((tokens, padded)),
            ],
            scratch_shapes=[pltpu.VMEM((tokens, lows[0].shape[1]), f32)],
        ),
        out_shape=[
            jax.ShapeDtypeStruct((1, 3, tokens, 2 * columns), bf16),
            jax.ShapeDtypeStruct((tokens, padded), bf16),
        ],
        compiler_params=params(24),
        name="embed",
    )(place, patch, position, rows, gains, *[weight] * SOURCE_PARTS, *lows)


def second_kernel(inputs_ref, gains_ref, *refs):
    weights, out_ref = refs[:SOURCE_PARTS], refs[-1]
    project_heads(pl.program_id(0), inputs_ref, weights, gains_ref, out_ref)


def second_half(inputs, weight, gains, out):
    tokens = inputs.shape[0]
    columns = weight.shape[2]
    return pl.pallas_call(
        second_kernel,
        grid=(3,),
        in_specs=[whole(inputs.shape), whole(gains.shape)]
        + weight_blocks(weight, 0)
        + [pl.BlockSpec(memory_space=pl.ANY)],
        out_specs=pl.BlockSpec((1, 1, tokens, columns), lambda i: (0, i, 0, 1)),
        out_shape=jax.ShapeDtypeStruct(out.shape, bf16),
        input_output_aliases={2 + SOURCE_PARTS: 0},
        compiler_params=params(24),
        name="second_half",
    )(inputs, gains, *[weight] * SOURCE_PARTS, out)


def turned(block, axis, step):
    count = lax.axis_size(axis)
    return lax.ppermute(block, axis, [(i, (i + step) % count) for i in range(count)])


def after(value, *others):
    return lax.optimization_barrier((value, others))[0]


def arrange_kernel(slab, patch_ref, position_ref, modulation_ref, patch_out, position_out, rows_out):
    shards = patch_ref.shape[1] // (2 * slab)
    stride = patch_out.shape[1] // shards
    patch_out[...] = jnp.zeros(patch_out.shape, bf16)
    position_out[...] = jnp.zeros(position_out.shape, bf16)
    rows_out[...] = jnp.zeros(rows_out.shape, f32)
    for index in range(shards):
        for side in range(2):
            old = slice((side * shards + index) * slab, (side * shards + index + 1) * slab)
            new = slice(index * stride + side * slab, index * stride + side * slab + slab)
            patch_out[:, new] = patch_ref[:, old]
            position_out[:, new] = position_ref[:, old]
            rows_out[0:2, new] = modulation_ref[0, 3:5, old]
            rows_out[2:3, new] = jnp.ones((1, slab), f32)


def arrange(slab, patch, position, modulation):
    depth = patch.shape[1]
    padded = depth // (2 * slab) * padded_rows(2 * slab)
    return pl.pallas_call(
        functools.partial(arrange_kernel, slab),
        out_shape=[
            jax.ShapeDtypeStruct((patch.shape[0], padded), bf16),
            jax.ShapeDtypeStruct((position.shape[0], padded), bf16),
            jax.ShapeDtypeStruct((8, padded), f32),
        ],
        compiler_params=params(12),
        name="arrange",
    )(patch, position, modulation)


def local(
    query,
    key,
    value,
    text_key,
    text_value,
    stream,
    modulation,
    out_weight,
    final_weight,
    final_bias,
    latents,
    sigmas,
    step_index,
    patch_weight,
    position,
    qkv_weight,
    norm_gains,
):
    zs, us = lax.axis_size("z"), lax.axis_size("uly")
    z, u = lax.axis_index("z"), lax.axis_index("uly")
    side, core = lax.axis_index("yh"), lax.axis_index("core")
    place = jnp.stack([u, side, core]).astype(jnp.int32)
    head = (zs * u + z).astype(jnp.int32).reshape(1)
    rows = query.shape[1]
    kinds, slab, columns = qkv_weight.shape

    branch = jnp.stack([step_index[0], lax.axis_index("cfg").astype(jnp.int32)])

    next_other = turned(qkv_weight, "yh", 1)
    out_other = turned(out_weight, "yh", 1)
    send, text = pack(zs, us, head, query, key, value, text_key, text_value)
    pieces = lax.all_to_all(send, ("z", "uly"), split_axis=0, concat_axis=0, tiled=True)

    own = pieces[:, :rows, :].reshape(zs * us * rows, 128)
    beside = turned(own, "core", 1)
    across = turned(own, "yh", 1)

    one, two = bundle(place[1:2], out_weight, out_other, qkv_weight, next_other)
    base = one.shape[0] - two.shape[0]
    one, two = after((one, two), pieces)
    sources = 2 * zs
    one_all = lax.all_gather(one, ("z", "core"), axis=0, tiled=True).reshape((sources,) + one.shape)
    two_all = lax.all_gather(two, ("z", "core"), axis=0, tiled=True).reshape((sources,) + two.shape)

    queries, peak, mixed = first_attend(text_key.shape[1], pieces, text, own, beside)
    across = after(across, peak)
    diagonal = turned(across, "core", 1)
    sent = last_attend(zs, queries, peak, mixed, across, diagonal)
    attended = lax.all_to_all(sent, "z", split_axis=0, concat_axis=0, tiled=True)
    parts = list(project(us, out_weight.shape[1], place, attended, one_all, base))
    parts[1:] = [turned(parts[step], "uly", step) for step in range(1, us)]

    patch, spots, one_all = after((patch_weight, position, one_all), parts[0])
    first_half = one_all[:, base:, :]
    patch, spots, shifts = arrange(slab, patch, spots, modulation)
    gains = jnp.concatenate([norm_gains, norm_gains], axis=1)
    predicted = predict(
        stream, modulation, final_weight, final_bias.reshape(1, -1), [parts], [patch, spots, shifts, gains, first_half]
    )
    partner = turned(predicted, "cfg", 1)
    velocity, latents_next, latents_low = euler(branch, sigmas, predicted, partner, latents)

    lows = [latents_low] + [turned(latents_low, "uly", step) for step in range(1, us)]
    half_qkv, inputs = embed(patch_weight.shape[1], place, lows, patch, spots, shifts, first_half, 0, gains)
    next_qkv = second_half(inputs, after(two_all, inputs), gains, half_qkv)
    return (velocity, latents_next, next_qkv)


def solution(mesh):
    sizes = dict(mesh.shape)
    fine = Mesh(
        mesh.devices.reshape(sizes["cfg"], 2, sizes["blk"] // 4, 2, sizes["uly"]),
        ("cfg", "yh", "z", "core", "uly"),
    )
    blk = ("yh", "z", "core")
    tokens = blk + ("uly",)
    placed = (
        P("cfg", tokens, None),
        P("cfg", tokens, None),
        P("cfg", tokens, None),
        P("cfg", None, None),
        P("cfg", None, None),
        P("cfg", tokens, None),
        P("cfg", None, None),
        P(("uly",) + blk, None),
        P(),
        P(),
        P(tokens, None),
        P(),
        P(),
        P(),
        P(blk, None),
        P(None, blk, "uly"),
        P(),
    )
    return jax.shard_map(
        local,
        mesh=fine,
        in_specs=placed,
        out_specs=(P(tokens, None), P(tokens, None), P("cfg", None, blk, "uly")),
        check_vma=False,
    )
```

```python
import functools

import jax
import jax.numpy as jnp
from jax import lax
from jax.experimental import pallas as pl
from jax.experimental.pallas import tpu as pltpu
from jax.sharding import Mesh, PartitionSpec as P

HD = 64
norm_epsilon = 1e-06
guidance_scale = 3.5
bf16 = jnp.bfloat16
f32 = jnp.float32
KEY_BLOCK = 1024
WEIGHT_PARTS = 5
SOURCE_PARTS = 4


def params(limit_mib, **more):
    return pltpu.CompilerParams(vmem_limit_bytes=limit_mib * 2**20, **more)


def attention_cost(queries, keys):
    return pl.CostEstimate(
        flops=queries * keys * 1024, transcendentals=queries * keys, bytes_accessed=(queries + keys) * 512
    )


def whole(shape):
    return pl.BlockSpec(shape, lambda *_: (0,) * len(shape))


def half_swap(block):
    return pltpu.roll(block.astype(f32), 64, 1).astype(block.dtype)


def low_lanes(shape):
    return lax.broadcasted_iota(jnp.int32, shape, len(shape) - 1) < 64


def pack_kernel(zs, us, head_ref, query_ref, key_ref, value_ref, text_key_ref, text_value_ref, send_ref, text_ref):
    rows = query_ref.shape[1]
    half = rows // 2
    low = low_lanes((rows, 128))
    low_half = low_lanes((half, 128))
    for pair in range(zs * us // 2):
        lanes = slice(128 * pair, 128 * pair + 128)
        keys = key_ref[0, :, lanes]
        values = value_ref[0, :, lanes]
        queries = query_ref[0, :, lanes] * 0.125
        first, second = queries[:half], queries[half:]
        for odd in range(2):
            head = 2 * pair + odd
            place = (head % zs) * us + head // zs
            if odd:
                both = jnp.where(low, half_swap(keys), values)
                folded = jnp.where(low_half, half_swap(first), second)
            else:
                both = jnp.where(low, keys, half_swap(values))
                folded = jnp.where(low_half, first, half_swap(second))
            send_ref[place, :rows, :] = both
            send_ref[place, rows:, :] = folded
    odd_head = lax.rem(head_ref[0], 2) == 1
    text_rows = text_key_ref.shape[1]
    text_low = low_lanes((text_rows, 128))
    keys = text_key_ref[0]
    values = text_value_ref[0]
    both = jnp.where(
        text_low,
        jnp.where(odd_head, half_swap(keys), keys),
        jnp.where(odd_head, values, half_swap(values)),
    )
    text_ref[...] = jnp.zeros(text_ref.shape, bf16)
    text_ref[:text_rows, :] = both


def pack(zs, us, head, query, key, value, text_key, text_value):
    rows = query.shape[1]
    text_rows = text_key.shape[1]
    text_padded = -(-text_rows // 128) * 128
    text_spec = pl.BlockSpec((1, text_rows, 128), lambda i, head: (0, 0, head[0] // 2))
    return pl.pallas_call(
        functools.partial(pack_kernel, zs, us),
        grid_spec=pltpu.PrefetchScalarGridSpec(
            num_scalar_prefetch=1,
            grid=(1,),
            in_specs=[whole(query.shape), whole(key.shape), whole(value.shape), text_spec, text_spec],
            out_specs=[whole((zs * us, rows + rows // 2, 128)), whole((text_padded, 128))],
        ),
        out_shape=[
            jax.ShapeDtypeStruct((zs * us, rows + rows // 2, 128), bf16),
            jax.ShapeDtypeStruct((text_padded, 128), bf16),
        ],
        compiler_params=params(56),
        name="pack",
    )(head, query, key, value, text_key, text_value)


def values_and_ones(both):
    return jnp.where(low_lanes(both.shape), jnp.ones_like(both), both)


def weighted(both, weights):
    return lax.dot_general(
        values_and_ones(both), weights, (((0,), (0,)), ((), ())), preferred_element_type=f32
    )


def scores_of(both, queries):
    return lax.dot_general(both, queries, (((1,), (1,)), ((), ())), preferred_element_type=f32)


def fold(peak, mixed, both, queries):
    scores = scores_of(both, queries)
    new_peak = jnp.maximum(peak, jnp.max(scores, axis=0, keepdims=True))
    weights = jnp.exp(scores - new_peak).astype(bf16)
    mixed = mixed * jnp.exp(peak - new_peak) + weighted(both, weights)
    return new_peak, mixed


def fold_all(peak, mixed, both_refs, queries):
    for both_ref in both_refs:
        for start in range(0, both_ref.shape[0], KEY_BLOCK):
            peak, mixed = fold(peak, mixed, both_ref[start : start + KEY_BLOCK, :], queries)
    return peak, mixed


def first_kernel(text_count, pieces_ref, text_ref, own_ref, beside_ref, queries_ref, peak_ref, mixed_ref):
    count, height, _ = pieces_ref.shape
    half = height // 3
    folded = pieces_ref[:, 2 * half :, :].reshape(count * half, 128)
    low = low_lanes(folded.shape)
    zero = jnp.zeros_like(folded)
    first = jnp.where(low, folded, zero).reshape(count, half, 128)
    second = jnp.where(low, half_swap(folded), zero).reshape(count, half, 128)
    queries = jnp.concatenate([first, second], axis=1).reshape(count * 2 * half, 128)
    queries_ref[...] = queries
    text = text_ref[...]
    scores = scores_of(text, queries)
    kept = lax.broadcasted_iota(jnp.int32, scores.shape, 0) < text_count
    scores = jnp.where(kept, scores, -1e30)
    peak = jnp.max(scores, axis=0, keepdims=True)
    weights = jnp.exp(scores - peak).astype(bf16)
    mixed = weighted(text, weights)
    peak_ref[...], mixed_ref[...] = fold_all(peak, mixed, (own_ref, beside_ref), queries)


def first_attend(text_count, pieces, text, own, beside):
    count, height, _ = pieces.shape
    total = count * (height // 3) * 2
    return pl.pallas_call(
        functools.partial(first_kernel, text_count),
        out_shape=[
            jax.ShapeDtypeStruct((total, 128), bf16),
            jax.ShapeDtypeStruct((1, total), f32),
            jax.ShapeDtypeStruct((128, total), f32),
        ],
        compiler_params=params(56),
        cost_estimate=attention_cost(total, text.shape[0] + own.shape[0] + beside.shape[0]),
        name="attend_first",
    )(pieces, text, own, beside)


def last_kernel(queries_ref, peak_ref, mixed_ref, across_ref, diagonal_ref, out_ref):
    _, mixed = fold_all(peak_ref[...], mixed_ref[...], (across_ref, diagonal_ref), queries_ref[...])
    attended = (mixed[64:] / mixed[0:1]).astype(bf16)
    width = out_ref.shape[2]
    for place in range(out_ref.shape[0]):
        out_ref[place] = attended[:, place * width : place * width + width]


def last_attend(zs, queries, peak, mixed, across, diagonal):
    total = queries.shape[0]
    return pl.pallas_call(
        last_kernel,
        out_shape=jax.ShapeDtypeStruct((zs, 64, total // zs), bf16),
        compiler_params=params(56),
        cost_estimate=attention_cost(total, across.shape[0] + diagonal.shape[0]),
        name="attend_last",
    )(queries, peak, mixed, across, diagonal)


def bundle_kernel(side_ref, out_ref, out_other_ref, next_ref, next_other_ref, first_ref, second_ref):
    low = side_ref[0] == 0

    def pair(own, other):
        return jnp.where(low, own, other), jnp.where(low, other, own)

    rows, width = out_ref.shape
    sets = -(-width // 256)
    for index in range(sets):
        lanes = slice(256 * index, min(256 * index + 256, width))
        count = lanes.stop - lanes.start
        for place, block in enumerate(pair(out_ref[:, lanes], out_other_ref[:, lanes])):
            start = (2 * index + place) * rows
            if count < 256:
                first_ref[start : start + rows, :] = jnp.zeros((rows, 256), bf16)
            first_ref[start : start + rows, :count] = block
    kinds, slab, _ = next_ref.shape
    padded = padded_rows(2 * slab)
    for half, target in enumerate((first_ref, second_ref)):
        base = target.shape[0] - kinds * padded
        lanes = slice(256 * half, 256 * half + 256)
        for kind in range(kinds):
            start = base + kind * padded
            target[start : start + padded, :] = jnp.zeros((padded, 256), bf16)
            for place, block in enumerate(pair(next_ref[kind, :, lanes], next_other_ref[kind, :, lanes])):
                target[start + place * slab : start + place * slab + slab, :] = block


def padded_rows(rows):
    return -(-rows // 16) * 16


def bundle(place, out_weight, out_other, next_weight, next_other):
    rows, width = out_weight.shape
    kinds, slab, columns = next_weight.shape
    second = kinds * padded_rows(2 * slab)
    first = 2 * rows * -(-width // 256) + second
    block = pl.BlockSpec(memory_space=pltpu.VMEM)
    return pl.pallas_call(
        bundle_kernel,
        in_specs=[pl.BlockSpec(memory_space=pltpu.SMEM)] + [block] * 4,
        out_specs=[block] * 2,
        out_shape=[jax.ShapeDtypeStruct((count, columns // 2), bf16) for count in (first, second)],
        compiler_params=params(8),
        name="bundle",
    )(place, out_weight, out_other, next_weight, next_other)


def project_kernel(place_ref, attended_ref, *refs):
    weights, outs, held = refs[:WEIGHT_PARTS], refs[WEIGHT_PARTS:-1], refs[-1]
    heads, _, tokens = attended_ref.shape
    sources, rows, _ = weights[0].shape
    slab = heads * 64 // (2 * sources)
    blocks = attended_ref[...].reshape(2, sources, slab, tokens)
    attended = jnp.concatenate([blocks[side, source] for source in range(sources) for side in range(2)], axis=0)
    attended = jnp.transpose(attended)
    width = held.shape[1]
    sets = rows // (2 * slab)
    for index in range(WEIGHT_PARTS * sets):
        start = index % sets * 2 * slab
        part = weights[index // sets][:, start : start + 2 * slab, :].reshape(heads * 64, 256)
        lanes = slice(256 * index, min(256 * index + 256, width))
        count = lanes.stop - lanes.start
        held[:, lanes] = jnp.dot(attended, part[:, :count], preferred_element_type=f32).astype(bf16)
    count = len(outs)
    size = tokens // count
    for order, out_ref in enumerate(outs):
        start = pl.multiple_of(lax.rem(place_ref[0] + order, count) * size, size)
        out_ref[...] = held[pl.ds(start, size), :]


def project(us, width, place, attended, bundles, base):
    tokens = attended.shape[2]
    piece = (tokens // us, width)
    part = (bundles.shape[0], base // WEIGHT_PARTS, 256)
    return pl.pallas_call(
        project_kernel,
        grid_spec=pltpu.PrefetchScalarGridSpec(
            num_scalar_prefetch=1,
            grid=(1,),
            in_specs=[whole(attended.shape)]
            + [pl.BlockSpec(part, functools.partial(lambda at, i, place: (0, at, 0), at)) for at in range(WEIGHT_PARTS)],
            out_specs=[whole(piece)] * us,
            scratch_shapes=[pltpu.VMEM((tokens, width), bf16)],
        ),
        out_shape=[jax.ShapeDtypeStruct(piece, bf16)] * us,
        compiler_params=params(24),
        name="project",
    )(place, attended, *[bundles] * WEIGHT_PARTS)


def layer_norm(matrix):
    mean = jnp.mean(matrix, axis=-1, keepdims=True)
    centred = matrix - mean
    variance = jnp.mean(centred * centred, axis=-1, keepdims=True)
    return centred * lax.rsqrt(variance + norm_epsilon)


def predict_kernel(parts, held, stream_ref, modulation_ref, weight_ref, bias_ref, *refs):
    pieces, out_ref = refs[: len(refs) - 1 - held], refs[-1]
    count = len(pieces) // parts
    gate = modulation_ref[0, 0:1, :]
    shift = modulation_ref[0, 1:2, :]
    scale = modulation_ref[0, 2:3, :]
    size = out_ref.shape[0] // parts
    for part in range(parts):
        projected = pieces[part * count][...].astype(f32)
        for piece in pieces[part * count + 1 : part * count + count]:
            projected += piece[...].astype(f32)
        rows = slice(part * size, part * size + size)
        residual = stream_ref[0, rows, :].astype(f32) + gate * projected
        normed = (layer_norm(residual) * (1.0 + scale) + shift).astype(bf16)
        out_ref[rows, :] = jnp.dot(normed, weight_ref[...], preferred_element_type=f32) + bias_ref[...]


def predict(stream, modulation, weight, bias, parts, held):
    pieces = [piece for part in parts for piece in part]
    block = pl.BlockSpec(memory_space=pltpu.VMEM)
    return pl.pallas_call(
        functools.partial(predict_kernel, len(parts), len(held)),
        in_specs=[block] * (4 + len(pieces)) + [pl.BlockSpec(memory_space=pl.ANY)] * len(held),
        out_specs=block,
        out_shape=jax.ShapeDtypeStruct((stream.shape[1], weight.shape[1]), f32),
        compiler_params=params(12),
        name="predict",
    )(stream, modulation, weight, bias, *pieces, *held)


def euler_kernel(step_ref, sigmas_ref, own_ref, partner_ref, latents_ref, velocity_ref, next_ref, low_ref):
    own, partner = own_ref[...], partner_ref[...]
    first = step_ref[1] == 0
    with_text = jnp.where(first, own, partner)
    without_text = jnp.where(first, partner, own)
    velocity = without_text + guidance_scale * (with_text - without_text)
    moment = step_ref[0]
    moved = latents_ref[...] + (sigmas_ref[moment + 1] - sigmas_ref[moment]) * velocity
    velocity_ref[...] = velocity
    next_ref[...] = moved
    low_ref[...] = moved.astype(bf16)


def euler(step, sigmas, own, partner, latents):
    scalars = pl.BlockSpec(memory_space=pltpu.SMEM)
    block = pl.BlockSpec(memory_space=pltpu.VMEM)
    return pl.pallas_call(
        euler_kernel,
        in_specs=[scalars, scalars, block, block, block],
        out_specs=[block] * 3,
        out_shape=[jax.ShapeDtypeStruct(own.shape, kind) for kind in (f32, f32, bf16)],
        compiler_params=params(4),
        name="euler",
    )(step, sigmas, own, partner, latents)


def project_heads(kind, inputs_ref, weight_refs, gains_ref, out_ref):
    sources, rows, columns = weight_refs[0].shape
    depth = sources * rows
    product = jnp.zeros((inputs_ref.shape[0], columns), f32)
    for order, weight_ref in enumerate(weight_refs):
        part = inputs_ref[:, order * depth : order * depth + depth]
        product += jnp.dot(part, weight_ref[...].reshape(depth, columns), preferred_element_type=f32)

    @pl.when(kind < 2)
    def _():
        gain = jnp.where(kind == 0, gains_ref[0:1, :], gains_ref[1:2, :])
        low = low_lanes((product.shape[0], 128))
        for pair in range(columns // 128):
            lanes = slice(128 * pair, 128 * pair + 128)
            block = product[:, lanes]
            squares = block * block
            left = jnp.sum(jnp.where(low, squares, 0.0), axis=-1, keepdims=True)
            right = jnp.sum(jnp.where(low, 0.0, squares), axis=-1, keepdims=True)
            mean = jnp.where(low, left, right) * (1.0 / HD)
            out_ref[0, 0, :, lanes] = (block * lax.rsqrt(mean + norm_epsilon) * gain).astype(bf16)

    @pl.when(kind == 2)
    def _():
        out_ref[0, 0] = product.astype(bf16)


def embed_kernel(depth, place_ref, patch_ref, position_ref, rows_ref, gains_ref, *refs):
    weights, lows = refs[:SOURCE_PARTS], refs[SOURCE_PARTS:-3]
    out_ref, inputs, latents = refs[-3:]

    @pl.when(pl.program_id(0) == 0)
    def _():
        count = len(lows)
        size = lows[0].shape[0]
        for order, low_ref in enumerate(lows):
            start = pl.multiple_of(lax.rem(place_ref[0] + count - order, count) * size, size)
            latents[pl.ds(start, size), :] = low_ref[...].astype(f32)
        embedded = jnp.dot(
            latents[...].astype(bf16), patch_ref[...], preferred_element_type=f32
        ) + position_ref[...].astype(f32)
        mean = jnp.sum(embedded, axis=-1, keepdims=True) * (1.0 / depth)
        centred = (embedded - mean) * rows_ref[2:3, :]
        variance = jnp.sum(centred * centred, axis=-1, keepdims=True) * (1.0 / depth)
        base = centred * lax.rsqrt(variance + norm_epsilon)
        inputs[...] = (base * (1.0 + rows_ref[1:2, :]) + rows_ref[0:1, :]).astype(bf16)

    project_heads(pl.program_id(0), inputs, weights, gains_ref, out_ref)


def weight_blocks(weight, base):
    sources, total, columns = weight.shape
    each = (total - base) // 3
    shape = (sources // SOURCE_PARTS, each, columns)
    return [
        pl.BlockSpec(shape, functools.partial(lambda at, i, *_: (at, base // each + i, 0), at))
        for at in range(SOURCE_PARTS)
    ]


def embed(depth, place, lows, patch, position, rows, weight, base, gains):
    tokens, padded = position.shape
    columns = weight.shape[2]
    return pl.pallas_call(
        functools.partial(embed_kernel, depth),
        grid_spec=pltpu.PrefetchScalarGridSpec(
            num_scalar_prefetch=1,
            grid=(3,),
            in_specs=[whole(patch.shape), whole(position.shape), whole(rows.shape), whole(gains.shape)]
            + weight_blocks(weight, base)
            + [whole(low.shape) for low in lows],
            out_specs=[
                pl.BlockSpec((1, 1, tokens, columns), lambda i, place: (0, i, 0, 0)),
                whole((tokens, padded)),
            ],
            scratch_shapes=[pltpu.VMEM((tokens, lows[0].shape[1]), f32)],
        ),
        out_shape=[
            jax.ShapeDtypeStruct((1, 3, tokens, 2 * columns), bf16),
            jax.ShapeDtypeStruct((tokens, padded), bf16),
        ],
        compiler_params=params(24),
        name="embed",
    )(place, patch, position, rows, gains, *[weight] * SOURCE_PARTS, *lows)


def second_kernel(inputs_ref, gains_ref, *refs):
    weights, out_ref = refs[:SOURCE_PARTS], refs[-1]
    project_heads(pl.program_id(0), inputs_ref, weights, gains_ref, out_ref)


def second_half(inputs, weight, gains, out):
    tokens = inputs.shape[0]
    columns = weight.shape[2]
    return pl.pallas_call(
        second_kernel,
        grid=(3,),
        in_specs=[whole(inputs.shape), whole(gains.shape)]
        + weight_blocks(weight, 0)
        + [pl.BlockSpec(memory_space=pl.ANY)],
        out_specs=pl.BlockSpec((1, 1, tokens, columns), lambda i: (0, i, 0, 1)),
        out_shape=jax.ShapeDtypeStruct(out.shape, bf16),
        input_output_aliases={2 + SOURCE_PARTS: 0},
        compiler_params=params(24),
        name="second_half",
    )(inputs, gains, *[weight] * SOURCE_PARTS, out)


def turned(block, axis, step):
    count = lax.axis_size(axis)
    return lax.ppermute(block, axis, [(i, (i + step) % count) for i in range(count)])


def after(value, *others):
    return lax.optimization_barrier((value, others))[0]


def arrange_kernel(slab, patch_ref, position_ref, modulation_ref, patch_out, position_out, rows_out):
    shards = patch_ref.shape[1] // (2 * slab)
    stride = patch_out.shape[1] // shards
    patch_out[...] = jnp.zeros(patch_out.shape, bf16)
    position_out[...] = jnp.zeros(position_out.shape, bf16)
    rows_out[...] = jnp.zeros(rows_out.shape, f32)
    for index in range(shards):
        for side in range(2):
            old = slice((side * shards + index) * slab, (side * shards + index + 1) * slab)
            new = slice(index * stride + side * slab, index * stride + side * slab + slab)
            patch_out[:, new] = patch_ref[:, old]
            position_out[:, new] = position_ref[:, old]
            rows_out[0:2, new] = modulation_ref[0, 3:5, old]
            rows_out[2:3, new] = jnp.ones((1, slab), f32)


def arrange(slab, patch, position, modulation):
    depth = patch.shape[1]
    padded = depth // (2 * slab) * padded_rows(2 * slab)
    return pl.pallas_call(
        functools.partial(arrange_kernel, slab),
        out_shape=[
            jax.ShapeDtypeStruct((patch.shape[0], padded), bf16),
            jax.ShapeDtypeStruct((position.shape[0], padded), bf16),
            jax.ShapeDtypeStruct((8, padded), f32),
        ],
        compiler_params=params(12),
        name="arrange",
    )(patch, position, modulation)


def local(
    query,
    key,
    value,
    text_key,
    text_value,
    stream,
    modulation,
    out_weight,
    final_weight,
    final_bias,
    latents,
    sigmas,
    step_index,
    patch_weight,
    position,
    qkv_weight,
    norm_gains,
):
    zs, us = lax.axis_size("z"), lax.axis_size("uly")
    z, u = lax.axis_index("z"), lax.axis_index("uly")
    side, core = lax.axis_index("yh"), lax.axis_index("core")
    place = jnp.stack([u, side, core]).astype(jnp.int32)
    head = (zs * u + z).astype(jnp.int32).reshape(1)
    rows = query.shape[1]
    kinds, slab, columns = qkv_weight.shape

    branch = jnp.stack([step_index[0], lax.axis_index("cfg").astype(jnp.int32)])

    next_other = turned(qkv_weight, "yh", 1)
    out_other = turned(out_weight, "yh", 1)
    send, text = pack(zs, us, head, query, key, value, text_key, text_value)
    pieces = lax.all_to_all(send, ("z", "uly"), split_axis=0, concat_axis=0, tiled=True)

    own = pieces[:, :rows, :].reshape(zs * us * rows, 128)
    beside = turned(own, "core", 1)
    across = turned(own, "yh", 1)

    one, two = bundle(place[1:2], out_weight, out_other, qkv_weight, next_other)
    base = one.shape[0] - two.shape[0]
    one, two = after((one, two), pieces)
    sources = 2 * zs
    one_all = lax.all_gather(one, ("z", "core"), axis=0, tiled=True).reshape((sources,) + one.shape)
    two_all = lax.all_gather(two, ("z", "core"), axis=0, tiled=True).reshape((sources,) + two.shape)

    queries, peak, mixed = first_attend(text_key.shape[1], pieces, text, own, beside)
    across = after(across, peak)
    diagonal = turned(across, "core", 1)
    sent = last_attend(zs, queries, peak, mixed, across, diagonal)
    attended = lax.all_to_all(sent, "z", split_axis=0, concat_axis=0, tiled=True)
    out_rows = one_all[:, :base, :]
    parts = list(project(us, out_weight.shape[1], place, attended, out_rows, base))
    parts[1:] = [turned(parts[step], "uly", step) for step in range(1, us)]

    patch, spots, one_all = after((patch_weight, position, one_all), parts[0])
    first_half = one_all[:, base:, :]
    patch, spots, shifts = arrange(slab, patch, spots, modulation)
    gains = jnp.concatenate([norm_gains, norm_gains], axis=1)
    predicted = predict(
        stream, modulation, final_weight, final_bias.reshape(1, -1), [parts], [patch, spots, shifts, gains, first_half]
    )
    partner = turned(predicted, "cfg", 1)
    velocity, latents_next, latents_low = euler(branch, sigmas, predicted, partner, latents)

    lows = [latents_low] + [turned(latents_low, "uly", step) for step in range(1, us)]
    half_qkv, inputs = embed(patch_weight.shape[1], place, lows, patch, spots, shifts, first_half, 0, gains)
    next_qkv = second_half(inputs, after(two_all, inputs), gains, half_qkv)
    return (velocity, latents_next, next_qkv)


def solution(mesh):
    sizes = dict(mesh.shape)
    fine = Mesh(
        mesh.devices.reshape(sizes["cfg"], 2, sizes["blk"] // 4, 2, sizes["uly"]),
        ("cfg", "yh", "z", "core", "uly"),
    )
    blk = ("yh", "z", "core")
    tokens = blk + ("uly",)
    placed = (
        P("cfg", tokens, None),
        P("cfg", tokens, None),
        P("cfg", tokens, None),
        P("cfg", None, None),
        P("cfg", None, None),
        P("cfg", tokens, None),
        P("cfg", None, None),
        P(("uly",) + blk, None),
        P(),
        P(),
        P(tokens, None),
        P(),
        P(),
        P(),
        P(blk, None),
        P(None, blk, "uly"),
        P(),
    )
    return jax.shard_map(
        local,
        mesh=fine,
        in_specs=placed,
        out_specs=(P(tokens, None), P(tokens, None), P("cfg", None, blk, "uly")),
        check_vma=False,
    )
```
